32 devices in a mesh: gx: 4 (over z), gy: 4 (over x, core), gz: 2 (over y).
Axes of the slice: x: 2, y: 2, z: 4, core: 2. Of those that a mesh axis runs over, the one named last changes fastest.
Arguments:
- blocks: bfloat16 [8192, 64, 448], P(('gx', 'gy', 'gz')), may hold values from -1.1953125 to 1.1953125
- prolong: bfloat16 [8192, 4096], P(('gx', 'gy', 'gz')), may hold values from -0.75 to 0.75
- new_owner: int32 [8192], P(('gx', 'gy', 'gz')), may hold values from 0 to 31, as said below
- arrival: int32 [8192], P(('gx', 'gy', 'gz')), may hold values from 0 to 267, as said below
- columns: int32 [8192, 7], P(('gx', 'gy', 'gz')), may hold values from -1 to 639, as said below
- targets: int32 [8192, 7], P(('gx', 'gy', 'gz')), may hold values from 0 to 223, as said below
- ghost_lists: int32 [32, 6, 64], P(('gx', 'gy', 'gz')), may hold values from 0 to 255
- touched: int32 [32, 224], P(('gx', 'gy', 'gz')), may hold values from 0 to 63
Outputs:
- coarse: float32 [2048, 4096], P(('gx', 'gy', 'gz'))
The draws below stay inside these ranges and needn't reach their ends.
Inputs may be any that keep to these rules, and one draw needn't show every extreme that they name: `new_owner`: every row's new owner is in the same gz column (same gx and gy index); two devices adjacent along gz swap the same number of rows both ways, between 4 and 6, and some adjacent pair swaps exactly 6; every other pair of distinct devices of a column swaps exactly 2 rows each way; so every device holds 256 rows after the move. `arrival`: below 256: an old row of the same device that stays; else 256 + p * 6 + r, the row of rank r among those that the device of gz index p of the column hands over; every staying and every handed-over row is named once. `columns`: entry 0 is the row's own new local index; entry k >= 1 is -1, a local row below 256, or 256 + (k - 1) * 64 + q, the q-th block sent by the neighbour in direction k - 1, which then exists. `targets`: a value v * 32 + q names, for v = 0, a coarse block of the device itself, and for v >= 1 one owned by its neighbour in direction v - 1, which then exists.
All inputs are finite; a program needn't handle non-finite values.
Results may differ from the reference program's by a relative error of at most 0.0029.
Values may be sent and summed in bfloat16 or wider, within the bound.
A program may use at most 256 MiB of HBM per device.

```python
import jax
import jax.numpy as jnp
from jax import lax

B = 64
NBR = 7
ROWS_DEV = 256
ROWS = 8192
FAR = 2
CAP = 6
GCAP = 64
UCAP = 32
U_DEV = 224
CE_DEV = 64
CE = 2048
N_GX = 4
N_GY = 4
N_GZ = 2
DEVICES = 32


def neighbour_table_drawn():
    device_count = ROWS // ROWS_DEV
    device_ids = jnp.arange(device_count, dtype=jnp.int32)
    coords = [device_ids // (N_GY * N_GZ), device_ids // N_GZ % N_GY, device_ids % N_GZ]
    extents = [N_GX, N_GY, N_GZ]
    strides = [N_GY * N_GZ, N_GZ, 1]
    listed = []
    for facing in range(6):
        axis_pos = facing // 2
        orient = 1 - 2 * (facing % 2)
        shifted = coords[axis_pos] + orient
        inside = (shifted >= 0) & (shifted < extents[axis_pos])
        listed.append(jnp.where(inside, device_ids + orient * strides[axis_pos], -1))
    return jnp.stack(listed, axis=1).astype(jnp.int32)


def repartition_plan(key):
    device_count = ROWS // ROWS_DEV
    column_count = device_count // N_GZ
    key_counts, key_order, key_shuffle = jax.random.split(key, 3)
    near_counts = jax.random.randint(key_counts, (column_count, N_GZ - 1), 2 * FAR, CAP + 1)
    near_counts = near_counts.at[0, N_GZ - 2].set(CAP)
    layer_ids = jnp.arange(N_GZ, dtype=jnp.int32)
    layer_gap = layer_ids[:, None] - layer_ids[None, :]
    lower_layer = jnp.minimum(jnp.minimum(layer_ids[:, None], layer_ids[None, :]), N_GZ - 2)
    counts = jnp.where(jnp.abs(layer_gap)[None] == 1, near_counts[:, lower_layer], jnp.where(layer_gap[None] != 0, FAR, 0)).astype(jnp.int32)
    out_counts = counts.reshape(device_count, N_GZ)
    in_counts = jnp.transpose(counts, (0, 2, 1)).reshape(device_count, N_GZ)
    cumulative = jnp.cumsum(out_counts, axis=1)
    orders = jax.vmap(lambda subkey: jax.random.permutation(subkey, ROWS_DEV))(jax.random.split(key_order, device_count)).astype(jnp.int32)
    positions = jnp.arange(ROWS_DEV, dtype=jnp.int32)
    peer_at = jnp.sum((positions[None, :, None] >= cumulative[:, None, :]).astype(jnp.int32), axis=2)
    device_ids = jnp.arange(device_count, dtype=jnp.int32)
    column_base = device_ids - device_ids % N_GZ
    owner_at = jnp.where(peer_at < N_GZ, column_base[:, None] + peer_at, device_ids[:, None]).astype(jnp.int32)
    owner_ids = jnp.zeros((device_count, ROWS_DEV), jnp.int32).at[device_ids[:, None], orders].set(owner_at)
    kept_rows = owner_ids == device_ids[:, None]
    slot_rank = jnp.arange(CAP, dtype=jnp.int32)
    incoming = (slot_rank[None, None, :] < in_counts[:, :, None]).reshape(device_count, N_GZ * CAP)
    valid_slots = jnp.concatenate([kept_rows, incoming], axis=1)
    length = ROWS_DEV + N_GZ * CAP
    slot_codes = jnp.arange(length, dtype=jnp.int32)
    shuffled = jax.vmap(lambda subkey: jax.random.permutation(subkey, length))(jax.random.split(key_shuffle, device_count)).astype(jnp.int32)
    scores = jnp.where(valid_slots, shuffled, length + slot_codes[None, :])
    picked = jnp.argsort(scores, axis=1)[:, :ROWS_DEV].astype(jnp.int32)
    return (owner_ids.reshape(-1).astype(jnp.int32), picked.reshape(-1).astype(jnp.int32))


def draw_new_owner(key, part):
    owner_ids, picked = repartition_plan(jax.random.fold_in(key, 11))
    return owner_ids


def draw_arrival(key, part):
    owner_ids, picked = repartition_plan(jax.random.fold_in(key, 11))
    return picked


def draw_columns(key, part):
    neighbours = neighbour_table_drawn()
    key_kind, key_local, key_ghost = jax.random.split(jax.random.fold_in(key, 23), 3)
    row_ids = jnp.arange(ROWS, dtype=jnp.int32)
    own_index = (row_ids % ROWS_DEV)[:, None]
    kind_draw = jax.random.randint(key_kind, (ROWS, NBR - 1), 0, 20)
    local_rows = jax.random.randint(key_local, (ROWS, NBR - 1), 0, ROWS_DEV)
    ghost_slot = jax.random.randint(key_ghost, (ROWS, NBR - 1), 0, GCAP)
    facing = jnp.arange(NBR - 1, dtype=jnp.int32)[None, :]
    present = neighbours[row_ids // ROWS_DEV] >= 0
    ghost_index = ROWS_DEV + facing * GCAP + ghost_slot
    others = jnp.where(kind_draw == 0, -1, jnp.where(kind_draw < 8, jnp.where(present, ghost_index, -1), local_rows))
    lists = jnp.concatenate([own_index, others], axis=1).astype(jnp.int32)
    lists = lists.at[0, 1].set(-1)
    lists = lists.at[ROWS_DEV, NBR - 1].set(ROWS_DEV + 6 * GCAP - 1)
    return lists


def draw_targets(key, part):
    neighbours = neighbour_table_drawn()
    key_dir, key_slot = jax.random.split(jax.random.fold_in(key, 31))
    row_ids = jnp.arange(ROWS, dtype=jnp.int32)
    pick_draw = jax.random.randint(key_dir, (ROWS,), 0, 12)
    facing = jnp.clip(pick_draw - 6, 0, 5)
    present = neighbours[row_ids // ROWS_DEV] >= 0
    matches = jnp.arange(6, dtype=jnp.int32)[None, :] == facing[:, None]
    has_peer = jnp.sum((matches & present).astype(jnp.int32), axis=1) > 0
    direction = jnp.where((pick_draw >= 6) & has_peer, facing + 1, 0)
    slot_draw = jax.random.randint(key_slot, (ROWS, NBR), 0, UCAP)
    result = direction[:, None] * UCAP + slot_draw
    result = result.at[ROWS_DEV].set(6 * UCAP + slot_draw[ROWS_DEV])
    result = result.at[ROWS_DEV, 0].set(7 * UCAP - 1)
    result = result.at[0, 0].set(0)
    return result.astype(jnp.int32)


def set_ends(values, key, low, largest):
    extent = values.shape
    place = [jax.random.randint(jax.random.fold_in(key, axis), (), 0, extent[axis]) for axis in range(len(extent))]
    values = values.at[tuple(place)].set(low)
    longest = extent.index(max(extent))
    place[longest] = (place[longest] + 1) % extent[longest]
    return values.at[tuple(place)].set(largest)


def block_levels(key, shape, pieces, smallest, largest):
    def one(dim, blocks):
        heights = jax.random.uniform(jax.random.fold_in(jax.random.fold_in(key, 6), dim), (blocks,), jnp.float32, smallest / len(pieces), largest / len(pieces))
        return jnp.repeat(jnp.exp(heights), shape[dim] // blocks).reshape((-1,) + (1,) * (len(shape) - dim - 1))

    loudness = one(*pieces[0])
    for cut in pieces[1:]:
        loudness = loudness * one(*cut)
    return loudness


def normal_values(own_key, extent, scale, reach, cuts=(), kind=jnp.bfloat16):
    gain = block_levels(own_key, extent, cuts, -0.22, 0.18) if cuts else 1.0
    drawn = jax.random.normal(own_key, extent, jnp.float32) * scale * gain
    return jnp.minimum(jnp.maximum(drawn, -reach), reach).astype(kind)


def setup_inputs(seed: int = 0) -> dict:
    seeds = jax.random.split(jax.random.key(seed), 9)
    blocks = normal_values(seeds[0], (ROWS, B, NBR * B), 0.2, 1.1953125, ((0, 32),))
    prolong = normal_values(seeds[1], (ROWS, B * B), B ** -0.5, 0.75, ((0, 32),))
    new_owner = draw_new_owner(jax.random.fold_in(seeds[8], 71), 0)
    arrival = draw_arrival(jax.random.fold_in(seeds[8], 71), 0)
    columns = draw_columns(jax.random.fold_in(seeds[8], 71), 0)
    targets = draw_targets(jax.random.fold_in(seeds[8], 71), 0)
    ghost_lists = set_ends(jax.random.randint(seeds[6], (DEVICES, 6, GCAP), 0, ROWS_DEV), jax.random.fold_in(seeds[6], 1), 0, ROWS_DEV - 1).astype(jnp.int32)
    touched = set_ends(jax.random.randint(seeds[7], (DEVICES, U_DEV), 0, CE_DEV), jax.random.fold_in(seeds[7], 1), 0, CE_DEV - 1).astype(jnp.int32)
    return {"blocks": blocks, "prolong": prolong, "new_owner": new_owner, "arrival": arrival, "columns": columns, "targets": targets, "ghost_lists": ghost_lists, "touched": touched}


def rank_within(labels, label_count):
    onehot = (labels[:, None] == jnp.arange(label_count, dtype=jnp.int32)[None, :]).astype(jnp.int32)
    before = jnp.cumsum(onehot, axis=0) - onehot
    return jnp.sum(before * onehot, axis=1).astype(jnp.int32)


def neighbour_table(device_count):
    device_ids = jnp.arange(device_count, dtype=jnp.int32)
    coords = [device_ids // (N_GY * N_GZ), (device_ids // N_GZ) % N_GY, device_ids % N_GZ]
    extents = [N_GX, N_GY, N_GZ]
    strides = [N_GY * N_GZ, N_GZ, 1]
    listed = []
    for facing in range(6):
        axis_pos = facing // 2
        orient = 1 - 2 * (facing % 2)
        shifted = coords[axis_pos] + orient
        inside = (shifted >= 0) & (shifted < extents[axis_pos])
        listed.append(jnp.where(inside, device_ids + orient * strides[axis_pos], -1))
    return jnp.stack(listed, axis=1).astype(jnp.int32)


def reference(blocks, prolong, new_owner, arrival, columns, targets, ghost_lists, touched):
    device_count = ROWS // ROWS_DEV
    neighbours = neighbour_table(device_count)
    row_ids = jnp.arange(ROWS, dtype=jnp.int32)
    source = (row_ids // ROWS_DEV).astype(jnp.int32)
    source_layer = (source % N_GZ).astype(jnp.int32)
    peer_layer = (new_owner % N_GZ).astype(jnp.int32)
    row_ranks = jax.vmap(lambda labels: rank_within(labels, N_GZ))(peer_layer.reshape(device_count, ROWS_DEV)).reshape(-1)
    table_size = device_count * N_GZ * CAP
    moved_rows = new_owner != source
    slot_key = jnp.where(moved_rows, (new_owner * N_GZ + source_layer) * CAP + row_ranks, table_size).astype(jnp.int32)
    inverse = jnp.zeros((table_size + 1,), jnp.int32).at[slot_key].set(row_ids)
    offset = jnp.maximum(arrival - ROWS_DEV, 0).astype(jnp.int32)
    lookup = ((source * N_GZ + offset // CAP) * CAP + offset % CAP).astype(jnp.int32)
    anchor = jnp.where(arrival < ROWS_DEV, source * ROWS_DEV + arrival, inverse[lookup]).astype(jnp.int32)
    arrived = blocks[anchor].reshape(device_count, ROWS_DEV, B, NBR * B)
    opposite = jnp.bitwise_xor(jnp.arange(6, dtype=jnp.int32), 1)
    slot_dir = (jnp.arange(U_DEV, dtype=jnp.int32) // UCAP).astype(jnp.int32)

    def one_device(coarse, inputs):
        rows_here, prolong_here, columns_here, targets_here, partners, touched_here, device_id = inputs
        safe_partners = jnp.maximum(partners, 0).astype(jnp.int32)
        ghost_index = (safe_partners[:, None] * ROWS_DEV + ghost_lists[safe_partners, opposite]).astype(jnp.int32)
        ghost_rows = prolong[ghost_index.reshape(-1)].reshape(6, GCAP, B * B)
        ghost_rows = jnp.where((partners >= 0)[:, None, None], ghost_rows, jnp.zeros((), prolong.dtype))
        block_table = jnp.concatenate([prolong_here, ghost_rows.reshape(-1, B * B)], axis=0).reshape(-1, B, B)
        live_mask = (columns_here >= 0).astype(jnp.float32)
        neighbour = block_table[jnp.maximum(columns_here, 0).astype(jnp.int32)]
        own_block = prolong_here.reshape(ROWS_DEV, B, B).astype(jnp.float32)
        left = jnp.einsum("rba,rbx->rax", own_block, rows_here.astype(jnp.float32), precision=lax.Precision.HIGHEST).astype(jnp.bfloat16)
        left = lax.optimization_barrier(left)
        left = left.reshape(ROWS_DEV, B, NBR, B).astype(jnp.float32)
        partial_blocks = jnp.einsum("rakb,rkbc->rkac", left, neighbour.astype(jnp.float32), precision=lax.Precision.HIGHEST)
        partial_blocks = partial_blocks * live_mask[:, :, None, None]
        slot_sums = jnp.zeros((U_DEV, B * B), jnp.float32).at[targets_here.reshape(-1).astype(jnp.int32)].add(partial_blocks.reshape(-1, B * B))
        owner_ids = jnp.where(slot_dir == 0, device_id, partners[jnp.clip(slot_dir - 1, 0, 5)]).astype(jnp.int32)
        has_owner = owner_ids >= 0
        entries = jnp.where(has_owner, owner_ids * CE_DEV + touched_here, 0).astype(jnp.int32)
        slot_sums = slot_sums * has_owner[:, None].astype(jnp.float32)
        coarse = coarse.at[entries].add(slot_sums)
        return coarse, None

    inputs = (arrived, prolong.reshape(device_count, ROWS_DEV, B * B), columns.reshape(device_count, ROWS_DEV, NBR), targets.reshape(device_count, ROWS_DEV, NBR), neighbours, touched, jnp.arange(device_count, dtype=jnp.int32))
    coarse, unused = lax.scan(one_device, jnp.zeros((CE, B * B), jnp.float32), inputs)
    return coarse
```

```python
import functools

import jax
import jax.numpy as jnp
from jax import lax
from jax.experimental import pallas as pl
from jax.experimental.pallas import tpu as pltpu
from jax.sharding import PartitionSpec as P

B = 64
NBR = 7
CAP = 6
AXES = ("gx", "gy", "gz")
FACES = 6
MESH = pl.DeviceIdType.MESH
VMEM_LIMIT = 60 * 1024 * 1024
ROW_CHUNKS = 8
ANY = pl.BlockSpec(memory_space=pl.ANY)
VMEM = pl.BlockSpec(memory_space=pltpu.VMEM)
SMEM = pl.BlockSpec(memory_space=pltpu.SMEM)


def face(direction):
    axis = AXES[direction // 2]
    there = lax.axis_index(axis) + (1 - 2 * (direction % 2))
    inside = (there >= 0) & (there < lax.axis_size(axis))
    return axis, there, inside


def pick_rows(index_ref, blocks_ref, out_ref, sems):
    copies = [
        pltpu.make_async_copy(blocks_ref.at[index_ref[s]], out_ref.at[s], sems.at[s])
        for s in range(out_ref.shape[0])
    ]
    for copy in copies:
        copy.start()
    for copy in copies:
        copy.wait()


def exchange_first(
    lists_ref, own_ref, leaving_ref, numbers_ref, ghost_ref, arriving_ref, got_ref,
    outbound, send_sem, recv_sem, num_send, num_recv, row_send, row_recv,
):
    layers = lax.axis_size("gz")
    layer = lax.axis_index("gz")
    barrier = pltpu.get_barrier_semaphore()
    expected = layers - 1
    for direction in range(4):
        axis, there, inside = face(direction)
        expected = expected + inside.astype(jnp.int32)

        @pl.when(inside)
        def _():
            pl.semaphore_signal(barrier, inc=1, device_id={axis: there}, device_id_type=MESH)

    for step in range(1, layers):
        pl.semaphore_signal(
            barrier, inc=1, device_id={"gz": lax.rem(layer + step, layers)}, device_id_type=MESH
        )
    pl.semaphore_wait(barrier, expected)

    def row_copy(step):
        target = lax.rem(layer + step, layers)
        return pltpu.make_async_remote_copy(
            src_ref=leaving_ref.at[pl.ds(target * CAP, CAP)],
            dst_ref=arriving_ref.at[pl.ds(layer * CAP, CAP)],
            send_sem=row_send.at[step - 1],
            recv_sem=row_recv.at[step - 1],
            device_id={"gz": target},
            device_id_type=MESH,
        )

    def ghost_copy(direction, axis, there):
        return pltpu.make_async_remote_copy(
            src_ref=outbound.at[direction],
            dst_ref=ghost_ref.at[direction ^ 1],
            send_sem=send_sem.at[direction],
            recv_sem=recv_sem.at[direction ^ 1],
            device_id={axis: there},
            device_id_type=MESH,
        )

    def number_copy(direction, axis, there):
        return pltpu.make_async_remote_copy(
            src_ref=numbers_ref.at[direction],
            dst_ref=got_ref.at[direction ^ 1],
            send_sem=num_send.at[direction],
            recv_sem=num_recv.at[direction ^ 1],
            device_id={axis: there},
            device_id_type=MESH,
        )

    for step in range(1, layers):
        row_copy(step).start()
    count = outbound.shape[1]
    for direction in (4, 5, 0, 1, 2, 3):

        def gather(q, carry, direction=direction):
            outbound[direction, q] = own_ref[lists_ref[direction * count + q]]
            return carry

        lax.fori_loop(0, count, gather, 0, unroll=8)
        axis, there, inside = face(direction)

        @pl.when(inside)
        def _():
            ghost_copy(direction, axis, there).start()
            number_copy(direction, axis, there).start()

    for direction in range(FACES):
        axis, there, inside = face(direction)

        @pl.when(inside)
        def _():
            ghost_copy(direction, axis, there).wait_send()
            number_copy(direction, axis, there).wait_send()
            ghost_copy(direction ^ 1, axis, there).wait_recv()
            number_copy(direction ^ 1, axis, there).wait_recv()

    for step in range(1, layers):
        row_copy(step).wait()


def product(
    arrival_ref, column_ref, target_ref, own_ref, ghost_ref, order_ref, blocks_ref, arriving_ref,
    kept_ref, sent_ref, table, rows, sum_a, sum_b, sems,
):
    row_count = rows.shape[0]
    chunk = row_count // ROW_CHUNKS

    def fetch(n, carry):
        a = arrival_ref[n]

        @pl.when(a < row_count)
        def _():
            pltpu.make_async_copy(blocks_ref.at[a], rows.at[n], sems.at[n // chunk]).start()

        @pl.when(a >= row_count)
        def _():
            pltpu.make_async_copy(
                arriving_ref.at[a - row_count], rows.at[n], sems.at[n // chunk]
            ).start()

        return carry

    lax.fori_loop(0, row_count, fetch, 0)
    low = lax.broadcasted_iota(jnp.int32, (B // 2, 2 * B), 1) < B
    low_full = lax.broadcasted_iota(jnp.int32, (B, 2 * B), 1) < B
    order = order_ref[...]

    def clear(u, carry):
        sum_a[u] = jnp.zeros(sum_a.shape[1:], jnp.float32)
        sum_b[u] = jnp.zeros(sum_b.shape[1:], jnp.float32)
        return carry

    lax.fori_loop(0, sum_a.shape[0], clear, 0, unroll=2)

    def unfold(source, base):
        def body(g, carry):
            parts = []
            for j in range(4):
                paired = source[4 * g + j].astype(jnp.float32)
                turned = pltpu.roll(paired, B, 1)
                parts.append(
                    jnp.concatenate(
                        [jnp.where(low, paired, turned), jnp.where(low, turned, paired)], axis=0
                    ).astype(jnp.bfloat16)
                )
            full = jnp.dot(
                order, jnp.concatenate(parts, axis=1), preferred_element_type=jnp.float32
            ).astype(jnp.bfloat16)
            for j in range(4):
                table[base + 4 * g + j] = full[:, 2 * B * j : 2 * B * (j + 1)]
            return carry

        lax.fori_loop(0, source.shape[0] // 4, body, 0, unroll=2)

    unfold(own_ref, 0)
    unfold(ghost_ref, row_count)
    table[table.shape[0] - 1] = jnp.zeros(table.shape[1:], jnp.bfloat16)
    zero = jnp.zeros((B, 2 * B), jnp.bfloat16)

    def one_row(n):
        left = lax.dot_general(
            table[n, :, :B], rows[n], (((0,), (0,)), ((), ())), preferred_element_type=jnp.float32
        ).astype(jnp.bfloat16)
        found = []
        for pair in range(NBR // 2):
            k = 2 * pair
            first = jnp.where(low_full, table[column_ref[n * NBR + k]], zero)
            second = jnp.where(low_full, zero, table[column_ref[n * NBR + k + 1]])
            found.append(
                jnp.dot(
                    left[:, B * k : B * (k + 2)],
                    jnp.concatenate([first, second], axis=0),
                    preferred_element_type=jnp.float32,
                )
            )
        k = NBR - 1
        found.append(
            jnp.dot(
                left[:, B * k :], table[column_ref[n * NBR + k]], preferred_element_type=jnp.float32
            )
        )
        for k in range(NBR):
            sums = (sum_a, sum_b)[k // 2 % 2]
            u = target_ref[n * NBR + k]
            half = slice(B * (k % 2), B * (k % 2 + 1))
            sums[u, :, half] = sums[u, :, half] + found[k // 2][:, half]

    def some_rows(c, carry):
        whole = rows.at[pl.ds(c * chunk, chunk)]
        pltpu.make_async_copy(whole, whole, sems.at[c]).wait()

        def body(i, inner):
            one_row(c * chunk + 2 * i)
            one_row(c * chunk + 2 * i + 1)
            return inner

        return lax.fori_loop(0, chunk // 2, body, carry)

    lax.fori_loop(0, ROW_CHUNKS, some_rows, 0)

    def folded(u):
        even = sum_a[u, pl.ds(0, B // 2, stride=2)] + sum_b[u, pl.ds(0, B // 2, stride=2)]
        odd = sum_a[u, pl.ds(1, B // 2, stride=2)] + sum_b[u, pl.ds(1, B // 2, stride=2)]
        return jnp.where(low, even + pltpu.roll(even, B, 1), odd + pltpu.roll(odd, B, 1))

    kept = kept_ref.shape[0]

    def keep(u, carry):
        kept_ref[u] = folded(u)
        return carry

    def hand_over(u, carry):
        sent_ref[u] = folded(u + kept).astype(jnp.bfloat16)
        return carry

    lax.fori_loop(0, kept, keep, 0, unroll=2)
    lax.fori_loop(0, sent_ref.shape[0], hand_over, 0, unroll=2)


def exchange_last(sent_ref, got_ref, send_sem, recv_sem):
    barrier = pltpu.get_barrier_semaphore()
    expected = 0
    for direction in range(FACES):
        axis, there, inside = face(direction)
        expected = expected + inside.astype(jnp.int32)

        @pl.when(inside)
        def _():
            pl.semaphore_signal(barrier, inc=1, device_id={axis: there}, device_id_type=MESH)

    pl.semaphore_wait(barrier, expected)

    def slot_copy(direction, axis, there):
        return pltpu.make_async_remote_copy(
            src_ref=sent_ref.at[direction],
            dst_ref=got_ref.at[direction ^ 1],
            send_sem=send_sem.at[direction],
            recv_sem=recv_sem.at[direction ^ 1],
            device_id={axis: there},
            device_id_type=MESH,
        )

    for direction in range(FACES):
        axis, there, inside = face(direction)

        @pl.when(inside)
        def _():
            slot_copy(direction, axis, there).start()

    for direction in range(FACES):
        axis, there, inside = face(direction)

        @pl.when(inside)
        def _():
            slot_copy(direction, axis, there).wait_send()
            slot_copy(direction ^ 1, axis, there).wait_recv()


def add_up(entry_ref, kept_ref, got_ref, coarse_ref, total):
    total[...] = jnp.zeros_like(total)
    kept = kept_ref.shape[0]

    def own(u, carry):
        e = entry_ref[u]
        total[e] = total[e] + kept_ref[u]
        return carry

    def other(u, carry):
        e = entry_ref[u + kept]
        total[e] = total[e] + got_ref[u].astype(jnp.float32)
        return carry

    lax.fori_loop(0, kept, own, 0, unroll=4)
    lax.fori_loop(0, got_ref.shape[0], other, 0, unroll=4)
    coarse_ref[...] = total[: coarse_ref.shape[0]]


def shards(entries, blocks, prolong, new_owner, arrival, columns, targets, ghost_lists, touched):
    row_count = blocks.shape[0]
    area = prolong.shape[1]
    layers = lax.axis_size("gz")
    layer = lax.axis_index("gz")
    ghosts = ghost_lists.shape[2]
    slots = touched.shape[1]
    share = slots // (FACES + 1)
    paired = (area // (2 * B), 2 * B)
    any_kernel = dict(vmem_limit_bytes=VMEM_LIMIT)

    peer = new_owner % layers
    row_ids = jnp.arange(row_count, dtype=jnp.int32)
    before = (peer[:, None] == peer[None, :]) & (row_ids[:, None] < row_ids[None, :])
    rank = jnp.sum(before.astype(jnp.int32), axis=0)
    key = jnp.where(peer == layer, -1, peer * CAP + rank)
    slot_ids = jnp.arange(layers * CAP, dtype=jnp.int32)
    chosen = jnp.sum(jnp.where(key[:, None] == slot_ids[None, :], row_ids[:, None], 0), axis=0)
    leaving = pl.pallas_call(
        pick_rows,
        out_shape=jax.ShapeDtypeStruct((layers * CAP,) + blocks.shape[1:], blocks.dtype),
        in_specs=[SMEM, ANY],
        out_specs=ANY,
        scratch_shapes=[pltpu.SemaphoreType.DMA((layers * CAP,))],
        name="pick_rows",
    )(chosen.astype(jnp.int32), blocks)

    own = prolong.reshape((row_count,) + paired)
    numbers = jnp.pad(touched.reshape(FACES + 1, 1, share)[1:], ((0, 0), (0, 7), (0, 128 - share)))
    ghost, arriving, got_numbers = pl.pallas_call(
        exchange_first,
        out_shape=[
            jax.ShapeDtypeStruct((FACES, ghosts) + paired, prolong.dtype),
            jax.ShapeDtypeStruct(leaving.shape, blocks.dtype),
            jax.ShapeDtypeStruct(numbers.shape, jnp.int32),
        ],
        in_specs=[SMEM, VMEM, ANY, ANY],
        out_specs=[ANY, ANY, ANY],
        scratch_shapes=[pltpu.VMEM((FACES, ghosts) + paired, prolong.dtype)]
        + [pltpu.SemaphoreType.DMA((FACES,))] * 4
        + [pltpu.SemaphoreType.DMA((layers - 1,))] * 2,
        compiler_params=pltpu.CompilerParams(
            collective_id=0, has_side_effects=True, **any_kernel
        ),
        name="exchange_first",
    )(ghost_lists.reshape(-1), own, leaving, numbers)

    place = jnp.arange(B, dtype=jnp.int32)
    order = (
        place[None, :] == (place[:, None] % 2) * (B // 2) + place[:, None] // 2
    ).astype(jnp.bfloat16)
    table_size = row_count + FACES * ghosts
    where = jnp.where(columns < 0, table_size, columns).reshape(-1)
    kept, sent = pl.pallas_call(
        product,
        out_shape=[
            jax.ShapeDtypeStruct((share,) + paired, jnp.float32),
            jax.ShapeDtypeStruct((FACES * share,) + paired, jnp.bfloat16),
        ],
        in_specs=[SMEM, SMEM, SMEM, VMEM, VMEM, VMEM, ANY, ANY],
        out_specs=[VMEM, VMEM],
        scratch_shapes=[
            pltpu.VMEM((table_size + 1, B, 2 * B), jnp.bfloat16),
            pltpu.VMEM(blocks.shape, blocks.dtype),
            pltpu.VMEM((slots, B, 2 * B), jnp.float32),
            pltpu.VMEM((slots, B, 2 * B), jnp.float32),
            pltpu.SemaphoreType.DMA((ROW_CHUNKS,)),
        ],
        compiler_params=pltpu.CompilerParams(**any_kernel),
        name="product",
    )(
        arrival, where, targets.reshape(-1), own, ghost.reshape((FACES * ghosts,) + paired),
        order, blocks, arriving,
    )

    got = pl.pallas_call(
        exchange_last,
        out_shape=jax.ShapeDtypeStruct((FACES, share) + paired, jnp.bfloat16),
        in_specs=[ANY],
        out_specs=ANY,
        scratch_shapes=[pltpu.SemaphoreType.DMA((FACES,))] * 2,
        compiler_params=pltpu.CompilerParams(collective_id=1, has_side_effects=True),
        name="exchange_last",
    )(sent.reshape((FACES, share) + paired))

    there = jnp.stack([face(direction)[2] for direction in range(FACES)])
    got_entry = jnp.where(there[:, None], got_numbers[:, 0, :share], entries).reshape(-1)
    entry = jnp.concatenate([touched[0, :share], got_entry])
    coarse = pl.pallas_call(
        add_up,
        out_shape=jax.ShapeDtypeStruct((entries,) + paired, jnp.float32),
        in_specs=[SMEM, VMEM, VMEM],
        out_specs=VMEM,
        scratch_shapes=[pltpu.VMEM((entries + 1,) + paired, jnp.float32)],
        name="add_up",
    )(entry, kept, got.reshape((FACES * share,) + paired))
    return coarse.reshape(entries, area)


ENTRIES = 64


def solution(mesh):
    rows = P(AXES)
    in_specs = (
        P(AXES, None, None), P(AXES, None), rows, rows,
        P(AXES, None), P(AXES, None), P(AXES, None, None), P(AXES, None),
    )
    return jax.shard_map(
        functools.partial(shards, ENTRIES),
        mesh=mesh,
        in_specs=in_specs,
        out_specs=P(AXES, None),
        check_vma=False,
    )
```

```python
import functools

import jax
import jax.numpy as jnp
from jax import lax
from jax.experimental import pallas as pl
from jax.experimental.pallas import tpu as pltpu
from jax.sharding import PartitionSpec as P

B = 64
NBR = 7
CAP = 6
AXES = ("gx", "gy", "gz")
FACES = 6
MESH = pl.DeviceIdType.MESH
VMEM_LIMIT = 60 * 1024 * 1024
ROW_CHUNKS = 8
ANY = pl.BlockSpec(memory_space=pl.ANY)
VMEM = pl.BlockSpec(memory_space=pltpu.VMEM)
SMEM = pl.BlockSpec(memory_space=pltpu.SMEM)


def face(direction):
    axis = AXES[direction // 2]
    there = lax.axis_index(axis) + (1 - 2 * (direction % 2))
    inside = (there >= 0) & (there < lax.axis_size(axis))
    return axis, there, inside


def pick_rows(index_ref, blocks_ref, out_ref, sems):
    copies = [
        pltpu.make_async_copy(blocks_ref.at[index_ref[s]], out_ref.at[s], sems.at[s])
        for s in range(out_ref.shape[0])
    ]
    for copy in copies:
        copy.start()
    for copy in copies:
        copy.wait()


def exchange_first(
    lists_ref, own_ref, leaving_ref, numbers_ref, ghost_ref, arriving_ref, got_ref,
    outbound, send_sem, recv_sem, num_send, num_recv, row_send, row_recv,
):
    layers = lax.axis_size("gz")
    layer = lax.axis_index("gz")
    barrier = pltpu.get_barrier_semaphore()
    expected = layers - 1
    for direction in range(4):
        axis, there, inside = face(direction)
        expected = expected + inside.astype(jnp.int32)

        @pl.when(inside)
        def _():
            pl.semaphore_signal(barrier, inc=1, device_id={axis: there}, device_id_type=MESH)

    for step in range(1, layers):
        pl.semaphore_signal(
            barrier, inc=1, device_id={"gz": lax.rem(layer + step, layers)}, device_id_type=MESH
        )
    pl.semaphore_wait(barrier, expected)

    def row_copy(step):
        target = lax.rem(layer + step, layers)
        return pltpu.make_async_remote_copy(
            src_ref=leaving_ref.at[pl.ds(target * CAP, CAP)],
            dst_ref=arriving_ref.at[pl.ds(layer * CAP, CAP)],
            send_sem=row_send.at[step - 1],
            recv_sem=row_recv.at[step - 1],
            device_id={"gz": target},
            device_id_type=MESH,
        )

    def ghost_copy(direction, axis, there):
        return pltpu.make_async_remote_copy(
            src_ref=outbound.at[direction],
            dst_ref=ghost_ref.at[direction ^ 1],
            send_sem=send_sem.at[direction],
            recv_sem=recv_sem.at[direction ^ 1],
            device_id={axis: there},
            device_id_type=MESH,
        )

    def number_copy(direction, axis, there):
        return pltpu.make_async_remote_copy(
            src_ref=numbers_ref.at[direction],
            dst_ref=got_ref.at[direction ^ 1],
            send_sem=num_send.at[direction],
            recv_sem=num_recv.at[direction ^ 1],
            device_id={axis: there},
            device_id_type=MESH,
        )

    for step in range(1, layers):
        row_copy(step).start()
    count = outbound.shape[1]
    for direction in (4, 5, 0, 1, 2, 3):

        def gather(q, carry, direction=direction):
            outbound[direction, q] = own_ref[lists_ref[direction * count + q]]
            return carry

        lax.fori_loop(0, count, gather, 0, unroll=8)
        axis, there, inside = face(direction)

        @pl.when(inside)
        def _():
            ghost_copy(direction, axis, there).start()
            number_copy(direction, axis, there).start()

    for direction in range(FACES):
        axis, there, inside = face(direction)

        @pl.when(inside)
        def _():
            ghost_copy(direction, axis, there).wait_send()
            number_copy(direction, axis, there).wait_send()
            ghost_copy(direction ^ 1, axis, there).wait_recv()
            number_copy(direction ^ 1, axis, there).wait_recv()

    for step in range(1, layers):
        row_copy(step).wait()


def product(
    arrival_ref, column_ref, target_ref, own_ref, ghost_ref, blocks_ref, arriving_ref,
    kept_ref, sent_ref, table, rows, sum_a, sum_b, sems,
):
    row_count = rows.shape[0]
    chunk = row_count // ROW_CHUNKS

    def fetch(n, carry):
        a = arrival_ref[n]

        @pl.when(a < row_count)
        def _():
            pltpu.make_async_copy(blocks_ref.at[a], rows.at[n], sems.at[n // chunk]).start()

        @pl.when(a >= row_count)
        def _():
            pltpu.make_async_copy(
                arriving_ref.at[a - row_count], rows.at[n], sems.at[n // chunk]
            ).start()

        return carry

    lax.fori_loop(0, row_count, fetch, 0, unroll=8)
    low = lax.broadcasted_iota(jnp.int32, (B // 2, 2 * B), 1) < B
    low_full = lax.broadcasted_iota(jnp.int32, (B, 2 * B), 1) < B
    place = lax.broadcasted_iota(jnp.int32, (B, B), 0)
    column = lax.broadcasted_iota(jnp.int32, (B, B), 1)
    order = jnp.where(
        column == (place & 1) * (B // 2) + (place >> 1), jnp.float32(1), jnp.float32(0)
    ).astype(jnp.bfloat16)

    def clear(u, carry):
        sum_a[u] = jnp.zeros(sum_a.shape[1:], jnp.float32)
        sum_b[u] = jnp.zeros(sum_b.shape[1:], jnp.float32)
        return carry

    lax.fori_loop(0, sum_a.shape[0], clear, 0, unroll=8)

    def unfold(source, base):
        def body(g, carry):
            parts = []
            for j in range(4):
                paired = source[4 * g + j].astype(jnp.float32)
                turned = pltpu.roll(paired, B, 1)
                parts.append(
                    jnp.concatenate(
                        [jnp.where(low, paired, turned), jnp.where(low, turned, paired)], axis=0
                    ).astype(jnp.bfloat16)
                )
            full = jnp.dot(
                order, jnp.concatenate(parts, axis=1), preferred_element_type=jnp.float32
            ).astype(jnp.bfloat16)
            for j in range(4):
                table[base + 4 * g + j] = full[:, 2 * B * j : 2 * B * (j + 1)]
            return carry

        lax.fori_loop(0, source.shape[0] // 4, body, 0, unroll=8)

    unfold(own_ref, 0)
    unfold(ghost_ref, row_count)
    table[table.shape[0] - 1] = jnp.zeros(table.shape[1:], jnp.bfloat16)
    zero = jnp.zeros((B, 2 * B), jnp.bfloat16)

    def entry(n, k):
        c = column_ref[k, n]
        return jnp.where(c < 0, table.shape[0] - 1, c)

    def some_rows_at(first):
        ns = [first + r for r in range(8)]
        lefts = [
            lax.dot_general(
                table[n, :, :B], rows[n], (((0,), (0,)), ((), ())), preferred_element_type=jnp.float32
            ).astype(jnp.bfloat16)
            for n in ns
        ]
        found = []
        for n, left in zip(ns, lefts):
            mine = []
            for k in range(0, NBR, 2):
                if k + 1 < NBR:
                    right = jnp.concatenate(
                        [
                            jnp.where(low_full, table[entry(n, k)], zero),
                            jnp.where(low_full, zero, table[entry(n, k + 1)]),
                        ],
                        axis=0,
                    )
                else:
                    right = table[entry(n, k)]
                mine.append(
                    jnp.dot(
                        left[:, B * k : B * (k + 2)], right, preferred_element_type=jnp.float32
                    )
                )
            found.append(mine)
        for n, mine in zip(ns, found):
            for k in range(NBR):
                sums = (sum_a, sum_b)[k // 2 % 2]
                u = target_ref[k, n]
                half = slice(B * (k % 2), B * (k % 2 + 1))
                sums[u, :, half] = sums[u, :, half] + mine[k // 2][:, half]

    def some_rows(c, carry):
        whole = rows.at[pl.ds(c * chunk, chunk)]
        pltpu.make_async_copy(whole, whole, sems.at[c]).wait()

        def body(i, inner):
            some_rows_at(c * chunk + 8 * i)
            return inner

        return lax.fori_loop(0, chunk // 8, body, carry)

    lax.fori_loop(0, ROW_CHUNKS, some_rows, 0)

    def folded(u):
        even = sum_a[u, pl.ds(0, B // 2, stride=2)] + sum_b[u, pl.ds(0, B // 2, stride=2)]
        odd = sum_a[u, pl.ds(1, B // 2, stride=2)] + sum_b[u, pl.ds(1, B // 2, stride=2)]
        return jnp.where(low, even + pltpu.roll(even, B, 1), odd + pltpu.roll(odd, B, 1))

    kept = kept_ref.shape[0]

    def keep(u, carry):
        kept_ref[u] = folded(u)
        return carry

    def hand_over(u, carry):
        sent_ref[u] = folded(u + kept).astype(jnp.bfloat16)
        return carry

    lax.fori_loop(0, kept, keep, 0, unroll=8)
    lax.fori_loop(0, sent_ref.shape[0], hand_over, 0, unroll=8)


def exchange_last(sent_ref, got_ref, send_sem, recv_sem):
    barrier = pltpu.get_barrier_semaphore()
    expected = 0
    for direction in range(FACES):
        axis, there, inside = face(direction)
        expected = expected + inside.astype(jnp.int32)

        @pl.when(inside)
        def _():
            pl.semaphore_signal(barrier, inc=1, device_id={axis: there}, device_id_type=MESH)

    pl.semaphore_wait(barrier, expected)

    def slot_copy(direction, axis, there):
        return pltpu.make_async_remote_copy(
            src_ref=sent_ref.at[direction],
            dst_ref=got_ref.at[direction ^ 1],
            send_sem=send_sem.at[direction],
            recv_sem=recv_sem.at[direction ^ 1],
            device_id={axis: there},
            device_id_type=MESH,
        )

    for direction in range(FACES):
        axis, there, inside = face(direction)

        @pl.when(inside)
        def _():
            slot_copy(direction, axis, there).start()

    for direction in range(FACES):
        axis, there, inside = face(direction)

        @pl.when(inside)
        def _():
            slot_copy(direction, axis, there).wait_send()
            slot_copy(direction ^ 1, axis, there).wait_recv()


def add_up(entry_ref, kept_ref, got_ref, coarse_ref, total):
    total[...] = jnp.zeros_like(total)
    kept = kept_ref.shape[0]

    def own(u, carry):
        e = entry_ref[u]
        total[e] = total[e] + kept_ref[u]
        return carry

    def other(u, carry):
        e = entry_ref[u + kept]
        total[e] = total[e] + got_ref[u].astype(jnp.float32)
        return carry

    lax.fori_loop(0, kept, own, 0, unroll=8)
    lax.fori_loop(0, got_ref.shape[0], other, 0, unroll=8)
    coarse_ref[...] = total[: coarse_ref.shape[0]]


def shards(entries, blocks, prolong, new_owner, arrival, columns, targets, ghost_lists, touched):
    row_count = blocks.shape[0]
    area = prolong.shape[1]
    layers = lax.axis_size("gz")
    layer = lax.axis_index("gz")
    ghosts = ghost_lists.shape[2]
    slots = touched.shape[1]
    share = slots // (FACES + 1)
    paired = (area // (2 * B), 2 * B)
    any_kernel = dict(vmem_limit_bytes=VMEM_LIMIT)

    peer = new_owner % layers
    row_ids = jnp.arange(row_count, dtype=jnp.int32)
    before = (peer[:, None] == peer[None, :]) & (row_ids[:, None] < row_ids[None, :])
    rank = jnp.sum(before.astype(jnp.int32), axis=0)
    key = jnp.where(peer == layer, -1, peer * CAP + rank)
    slot_ids = jnp.arange(layers * CAP, dtype=jnp.int32)
    chosen = jnp.sum(jnp.where(key[:, None] == slot_ids[None, :], row_ids[:, None], 0), axis=0)
    leaving = pl.pallas_call(
        pick_rows,
        out_shape=jax.ShapeDtypeStruct((layers * CAP,) + blocks.shape[1:], blocks.dtype),
        in_specs=[SMEM, ANY],
        out_specs=VMEM,
        scratch_shapes=[pltpu.SemaphoreType.DMA((layers * CAP,))],
        compiler_params=pltpu.CompilerParams(**any_kernel),
        name="pick_rows",
    )(chosen.astype(jnp.int32), blocks)

    own = prolong.reshape((row_count,) + paired)
    numbers = jnp.pad(touched.reshape(FACES + 1, 1, share)[1:], ((0, 0), (0, 7), (0, 128 - share)))
    ghost, arriving, got_numbers = pl.pallas_call(
        exchange_first,
        out_shape=[
            jax.ShapeDtypeStruct((FACES, ghosts) + paired, prolong.dtype),
            jax.ShapeDtypeStruct(leaving.shape, blocks.dtype),
            jax.ShapeDtypeStruct(numbers.shape, jnp.int32),
        ],
        in_specs=[SMEM, VMEM, ANY, ANY],
        out_specs=[ANY, ANY, ANY],
        scratch_shapes=[pltpu.VMEM((FACES, ghosts) + paired, prolong.dtype)]
        + [pltpu.SemaphoreType.DMA((FACES,))] * 4
        + [pltpu.SemaphoreType.DMA((layers - 1,))] * 2,
        compiler_params=pltpu.CompilerParams(
            collective_id=0, has_side_effects=True, **any_kernel
        ),
        name="exchange_first",
    )(ghost_lists.reshape(-1), own, leaving, numbers)

    table_size = row_count + FACES * ghosts
    kept, sent = pl.pallas_call(
        product,
        out_shape=[
            jax.ShapeDtypeStruct((share,) + paired, jnp.float32),
            jax.ShapeDtypeStruct((FACES * share,) + paired, jnp.bfloat16),
        ],
        in_specs=[SMEM, SMEM, SMEM, VMEM, VMEM, ANY, ANY],
        out_specs=[VMEM, VMEM],
        scratch_shapes=[
            pltpu.VMEM((table_size + 1, B, 2 * B), jnp.bfloat16),
            pltpu.VMEM(blocks.shape, blocks.dtype),
            pltpu.VMEM((slots, B, 2 * B), jnp.float32),
            pltpu.VMEM((slots, B, 2 * B), jnp.float32),
            pltpu.SemaphoreType.DMA((ROW_CHUNKS,)),
        ],
        compiler_params=pltpu.CompilerParams(**any_kernel),
        name="product",
    )(
        arrival, columns.T, targets.T, own, ghost.reshape((FACES * ghosts,) + paired),
        blocks, arriving,
    )

    got = pl.pallas_call(
        exchange_last,
        out_shape=jax.ShapeDtypeStruct((FACES, share) + paired, jnp.bfloat16),
        in_specs=[ANY],
        out_specs=ANY,
        scratch_shapes=[pltpu.SemaphoreType.DMA((FACES,))] * 2,
        compiler_params=pltpu.CompilerParams(collective_id=1, has_side_effects=True),
        name="exchange_last",
    )(sent.reshape((FACES, share) + paired))

    there = jnp.stack([face(direction)[2] for direction in range(FACES)])
    got_entry = jnp.where(there[:, None], got_numbers[:, 0, :share], entries).reshape(-1)
    entry = jnp.concatenate([touched[0, :share], got_entry])
    coarse = pl.pallas_call(
        add_up,
        out_shape=jax.ShapeDtypeStruct((entries,) + paired, jnp.float32),
        in_specs=[SMEM, VMEM, VMEM],
        out_specs=VMEM,
        scratch_shapes=[pltpu.VMEM((entries + 1,) + paired, jnp.float32)],
        name="add_up",
    )(entry, kept, got.reshape((FACES * share,) + paired))
    return coarse.reshape(entries, area)


ENTRIES = 64


def solution(mesh):
    rows = P(AXES)
    in_specs = (
        P(AXES, None, None), P(AXES, None), rows, rows,
        P(AXES, None), P(AXES, None), P(AXES, None, None), P(AXES, None),
    )
    return jax.shard_map(
        functools.partial(shards, ENTRIES),
        mesh=mesh,
        in_specs=in_specs,
        out_specs=P(AXES, None),
        check_vma=False,
    )
```
